512 devices in a mesh: blk: 128 (over x_lo, z, y), feat: 4 (over x_hi, core).
Axes of the slice: x: 4 (x_hi: 2, x_lo: 2; x = x_hi * 2 + x_lo), y: 8, z: 8, core: 2. Of those that a mesh axis runs over, the one named last changes fastest.
Arguments:
- points: bfloat16 [768, 262144], P('feat', 'blk'), as said below
- centroids: bfloat16 [768, 65536], P('feat', 'blk'), as said below
- col_pot: float32 [65536], P('blk'), may hold values from -9 to 9
- row_pot: float32 [262144], P('blk'), may hold values from -9 to 9
Outputs:
- row_lse: float32 [262144], P('blk')
- col_lse: float32 [65536], P(('blk', 'feat'))
- centroid_mean: float32 [65536, 768], P(('blk', 'feat'))
The draws below stay inside these ranges and needn't reach their ends.
Inputs may be any that keep to these rules, and one draw needn't show every extreme that they name: `centroids`: entries of order one. `points`: entries of order one.
All inputs are finite; a program needn't handle non-finite values.
Results may differ from the reference program's by a relative error of at most 0.0008.
Values may be sent and summed in bfloat16 or wider, within the bound.
No kernel may reach another device: no remote copies, remote signals or barrier semaphores. Data moves between devices by JAX's collectives and lax.ppermute only.
A program may use at most 64 MiB of HBM per device.

```python
import jax
import jax.numpy as jnp
from jax import lax

D = 768
ROWS_DEV = 2048
PANEL = 512
HOPS = 4
NPTS = 262144
K = 65536
N_BLK = 128


def centroid_base(key):
    return jax.random.normal(key, (K, D), jnp.float32)


def draw_centroids(key, part):
    shared = centroid_base(key)
    return shared.T.astype(jnp.bfloat16)


def draw_points(key, part):
    key = jax.random.fold_in(key, 5)
    values = jax.random.normal(key, (NPTS, D), jnp.float32)
    return values.T.astype(jnp.bfloat16)


def shard_levels(stream_key, shape, pieces, least, largest):
    def one(axis_at, shards_of):
        draws = jax.random.uniform(jax.random.fold_in(jax.random.fold_in(stream_key, 6), axis_at), (shards_of,), jnp.float32, least / len(pieces), largest / len(pieces))
        return jnp.repeat(jnp.exp(draws), shape[axis_at] // shards_of).reshape((-1,) + (1,) * (len(shape) - axis_at - 1))

    level = one(*pieces[0])
    for cut in pieces[1:]:
        level = level * one(*cut)
    return level


def scatter_about(stream_key, extent, deviation, most, cuts=(), kind=jnp.bfloat16):
    result = jax.random.normal(stream_key, extent, jnp.float32) * deviation
    if len(cuts) > 0:
        result = shard_levels(stream_key, extent, cuts, -0.22, 0.18) * result
    return jnp.clip(result, min=-most, max=most).astype(kind)


def setup_inputs(seed: int = 0) -> dict:
    key_of = jax.random.split(jax.random.key(seed), 5)
    return {
        "points": draw_points(jax.random.fold_in(key_of[4], 71), 0),
        "centroids": draw_centroids(jax.random.fold_in(key_of[4], 71), 0),
        "col_pot": scatter_about(key_of[2], (K,), 1.5, 9.0, ((0, 128),), jnp.float32),
        "row_pot": scatter_about(key_of[3], (NPTS,), 1.5, 9.0, ((0, 128),), jnp.float32),
    }


def merge_rows(first, second):
    top = jnp.maximum(first[0], second[0])
    return top, first[1] * jnp.exp(first[0] - top) + second[1] * jnp.exp(second[0] - top)


def merge_cols(first, second):
    top = jnp.maximum(first[0], second[0])
    left = jnp.exp(first[0] - top)
    right = jnp.exp(second[0] - top)
    return top, first[1] * left + second[1] * right, first[2] * left[:, None] + second[2] * right[:, None]


def pair_terms(block_points, panel_rows, potential, block_pot):
    squares = jnp.sum(jnp.square(panel_rows.astype(jnp.float32)), axis=1)
    dots = jnp.dot(block_points, panel_rows.T, preferred_element_type=jnp.float32)
    score = (dots - 0.5 * squares[None, :]) * (1.0 / (0.02 * D))
    row_terms = score + potential[None, :]
    row_max = jnp.max(row_terms, axis=1)
    row_sum = jnp.sum(jnp.exp(row_terms - row_max[:, None]), axis=1)
    col_terms = score - block_pot[:, None]
    col_max = jnp.max(col_terms, axis=0)
    expo = jnp.exp(col_terms - col_max[None, :])
    col_sum = jnp.sum(expo, axis=0)
    weight = expo.astype(jnp.bfloat16)
    col_acc = jnp.dot(weight.T, block_points, preferred_element_type=jnp.float32)
    return (row_max, row_sum), (col_max, col_sum, col_acc)


def reference(points, centroids, col_pot, row_pot):
    points = points.T
    centroids = centroids.T

    def one_panel(panel_index):
        panel_rows = lax.dynamic_slice_in_dim(centroids, panel_index * PANEL, PANEL, 0)
        potential = lax.dynamic_slice_in_dim(col_pot, panel_index * PANEL, PANEL, 0)
        row_maxes = []
        row_sums = []
        col_state = None
        for offset in range(HOPS + 1):
            block = ((panel_index + offset) % N_BLK).astype(jnp.int32)
            block_points = lax.dynamic_slice_in_dim(points, block * ROWS_DEV, ROWS_DEV, 0)
            block_pot = lax.dynamic_slice_in_dim(row_pot, block * ROWS_DEV, ROWS_DEV, 0)
            row_part, col_part = pair_terms(block_points, panel_rows, potential, block_pot)
            row_maxes.append(row_part[0])
            row_sums.append(row_part[1])
            col_state = col_part if col_state is None else merge_cols(col_state, col_part)
        col_lse = col_state[0] + jnp.log(col_state[1])
        centroid_mean = col_state[2] / col_state[1][:, None]
        return jnp.stack(row_maxes), jnp.stack(row_sums), col_lse, centroid_mean

    row_maxes, row_sums, col_lse, centroid_mean = lax.map(one_panel, jnp.arange(N_BLK, dtype=jnp.int32))
    row_state = None
    for offset in range(HOPS + 1):
        part = (jnp.roll(row_maxes[:, offset], offset, axis=0), jnp.roll(row_sums[:, offset], offset, axis=0))
        row_state = part if row_state is None else merge_rows(row_state, part)
    row_lse = (row_state[0] + jnp.log(row_state[1])).reshape(NPTS)
    return row_lse, col_lse.reshape(K), centroid_mean.reshape(K, D)
```

```python
import functools

import jax
import jax.numpy as jnp
from jax import lax
from jax.experimental import pallas as pl
from jax.experimental.pallas import tpu as pltpu
from jax.sharding import PartitionSpec as P

HOPS = 4
EXTRA = 16
CHUNK = 512
STAT = 128


def shifted(block, distance):
    size = lax.axis_size("blk")
    return lax.ppermute(block, "blk", [(i, (i + distance) % size) for i in range(size)])


def swapped(block, mask):
    size = lax.axis_size("feat")
    return lax.ppermute(block, "feat", [(i, i ^ mask) for i in range(size)])


def three_terms(value):
    high = value.astype(jnp.bfloat16).astype(jnp.float32)
    rest = value - high
    middle = rest.astype(jnp.bfloat16).astype(jnp.float32)
    return high, middle, rest - middle


def stat_lanes(lse):
    high, middle, low = three_terms(lse)
    lane = lax.broadcasted_iota(jnp.int32, (lse.shape[0], STAT), 1)
    return jnp.where(lane == 0, high, jnp.where(lane == 1, middle, jnp.where(lane == 2, low, 0.0)))


def split_kernel(cent, pot, *outs):
    member = lax.axis_index("feat")
    quarter = outs[0].shape[1]
    for mask in range(4):
        start = pl.multiple_of((member ^ mask) * quarter, quarter)
        outs[mask][...] = cent[:, pl.ds(start, quarter)]
    own = pot[:, pl.ds(pl.multiple_of(member * quarter, quarter), quarter)]
    high, middle, low = three_terms(own)
    row = lax.broadcasted_iota(jnp.int32, (EXTRA, quarter), 0)
    rows = jnp.where(row == 0, high, jnp.where(row == 1, middle, jnp.where(row == 2, low, 0.0)))
    outs[4][...] = rows.astype(jnp.bfloat16)


def split_panel(centroids, col_pot):
    depth, width = centroids.shape
    quarter = width // 4
    piece = jax.ShapeDtypeStruct((depth, quarter), centroids.dtype)
    return pl.pallas_call(
        split_kernel,
        out_shape=(piece,) * 4 + (jax.ShapeDtypeStruct((EXTRA, quarter), jnp.bfloat16),),
        name="split_panel",
    )(centroids, col_pot[None, :])


def pair_kernel(scale, first, *refs):
    pts = refs[:4]
    if first:
        panel, row_pot, packed, row_out, scores = refs[4:]
    else:
        panel, row_pot, row_in, packed, row_out, scores = refs[4:]
    depth, count = pts[0].shape
    features = 4 * depth
    turned = panel[...].T
    cols = turned[:, :features]
    extra = turned[:, features : features + 3].astype(jnp.float32)
    potential = jnp.sum(extra, axis=1, keepdims=True)
    wide = cols.astype(jnp.float32)
    bias = (-0.5 * scale) * jnp.sum(wide * wide, axis=1, keepdims=True)
    top = None
    for at in range(0, count, CHUNK):
        here = pl.ds(at, CHUNK)
        score = None
        for m in range(4):
            part = jnp.dot(
                cols[:, depth * m : depth * (m + 1)], pts[m][:, here], preferred_element_type=jnp.float32
            )
            score = part if score is None else score + part
        score = score * scale + bias
        row_terms = score + potential
        row_max = jnp.max(row_terms, axis=0, keepdims=True)
        row_sum = jnp.sum(jnp.exp(row_terms - row_max), axis=0, keepdims=True)
        row_part = row_max + jnp.log(row_sum)
        if not first:
            before = row_in[:, here]
            larger = jnp.maximum(before, row_part)
            row_part = larger + jnp.log(jnp.exp(before - larger) + jnp.exp(row_part - larger))
        row_out[:, here] = row_part
        col_terms = score - row_pot[:, here]
        scores[:, here] = col_terms
        for j in range(0, CHUNK, 128):
            lane_part = col_terms[:, j : j + 128]
            top = lane_part if top is None else jnp.maximum(top, lane_part)
    col_max = jnp.max(top, axis=1, keepdims=True)
    lane_sum = None
    acc = [None] * 4
    for at in range(0, count, CHUNK):
        here = pl.ds(at, CHUNK)
        expo = jnp.exp(scores[:, here] - col_max)
        for j in range(0, CHUNK, 128):
            lane_part = expo[:, j : j + 128]
            lane_sum = lane_part if lane_sum is None else lane_sum + lane_part
        weight = expo.astype(jnp.bfloat16)
        for m in range(4):
            part = lax.dot_general(
                weight, pts[m][:, here], (((1,), (1,)), ((), ())), preferred_element_type=jnp.float32
            )
            acc[m] = part if acc[m] is None else acc[m] + part
    col_sum = jnp.sum(lane_sum, axis=1, keepdims=True)
    inverse = 1.0 / col_sum
    for m in range(4):
        packed[:, depth * m : depth * (m + 1)] = acc[m] * inverse
    packed[:, features:] = stat_lanes(col_max + jnp.log(col_sum))


def pair(points, panel, row_pot, row_in, name):
    depth, count = points[0].shape
    features = 4 * depth
    quarter = panel.shape[1]
    operands = (*points, panel, row_pot) + (() if row_in is None else (row_in,))
    return pl.pallas_call(
        functools.partial(pair_kernel, 1.0 / (0.02 * features), row_in is None),
        out_shape=(
            jax.ShapeDtypeStruct((quarter, features + STAT), jnp.float32),
            jax.ShapeDtypeStruct((1, count), jnp.float32),
        ),
        scratch_shapes=[pltpu.VMEM((quarter, count), jnp.float32)],
        compiler_params=pltpu.CompilerParams(vmem_limit_bytes=24 * 2**20),
        cost_estimate=pl.CostEstimate(
            flops=4 * features * count * quarter, bytes_accessed=8 * 2**20, transcendentals=2 * count * quarter
        ),
        name=name,
    )(*operands)


def half(packed):
    return packed.astype(jnp.float16)


def whole(packed):
    return packed.astype(jnp.float32)


def merge_kernel(count, final, *refs):
    features = refs[0].shape[1] - STAT
    stats = [ref[:, features : features + 3] for ref in refs[:count]]
    lses = [jnp.sum(stat, axis=1, keepdims=True) for stat in stats]
    top = functools.reduce(jnp.maximum, lses)
    weights = [jnp.exp(lse - top) for lse in lses]
    total = functools.reduce(jnp.add, weights)
    inverse = 1.0 / total
    lse = top + jnp.log(total)
    mean = None
    for weight, ref in zip(weights, refs[:count]):
        part = ref[:, :features] * (weight * inverse)
        mean = part if mean is None else mean + part
    if not final:
        packed = refs[count]
        packed[:, :features] = mean
        packed[:, features:] = stat_lanes(lse)
        return
    mean_out, lse_out = refs[count:]
    lse_out[...] = jnp.broadcast_to(lse, (lse.shape[0], lse.shape[0])).T[:1, :]
    member = lax.axis_index("feat")
    depth = features // 4
    for at in range(4):

        @pl.when(member == at)
        def _():
            for m in range(4):
                mean_out[:, depth * (m ^ at) : depth * ((m ^ at) + 1)] = mean[:, depth * m : depth * (m + 1)]


def merge(parts, final, name):
    quarter, width = parts[0].shape
    if final:
        shapes = (
            jax.ShapeDtypeStruct((quarter, width - STAT), jnp.float32),
            jax.ShapeDtypeStruct((1, quarter), jnp.float32),
        )
    else:
        shapes = jax.ShapeDtypeStruct((quarter, width), jnp.float32)
    return pl.pallas_call(
        functools.partial(merge_kernel, len(parts), final),
        out_shape=shapes,
        cost_estimate=pl.CostEstimate(
            flops=2 * len(parts) * quarter * width,
            bytes_accessed=4 * (len(parts) + 1) * quarter * width,
            transcendentals=0,
        ),
        name=name,
    )(*parts)


def local(points, centroids, col_pot, row_pot):
    depth, count = points.shape
    features = 4 * depth
    member = lax.axis_index("feat")
    across = swapped(points, 2)
    pieces = split_panel(centroids, col_pot)
    panel0 = jnp.concatenate(
        [pieces[0]] + [swapped(pieces[mask], mask) for mask in (1, 2, 3)] + [pieces[4]], axis=0
    )
    beside = swapped(points, 1)
    panel1 = shifted(panel0, 1)
    panel4 = shifted(panel0, 4)
    panel2 = shifted(panel1, 1)
    diagonal = swapped(across, 1)
    panel3 = shifted(panel2, 1)
    full = (points, beside, across, diagonal)
    pot = row_pot[None, :]
    part4, rows = pair(full, panel4, pot, None, "pair4")
    back4 = shifted(half(part4), -4)
    part1, rows = pair(full, panel1, pot, rows, "pair1")
    back1 = shifted(half(part1), -1)
    part0, rows = pair(full, panel0, pot, rows, "pair0")
    part2, rows = pair(full, panel2, pot, rows, "pair2")
    part3, rows = pair(full, panel3, pot, rows, "pair3")
    back3 = whole(shifted(half(part3), -1))
    both = merge((part2, back3), False, "merge_pair")
    back2 = whole(shifted(half(both), -2))
    row_parts = lax.all_gather(rows[0], "feat")
    row_top = jnp.max(row_parts, axis=0)
    row_lse = row_top + jnp.log(jnp.sum(jnp.exp(row_parts - row_top[None, :]), axis=0))
    mean, col_lse = merge((part0, whole(back1), whole(back4), back2), True, "merge_last")
    return (row_lse, col_lse[0], mean)


def solution(mesh):
    return jax.shard_map(
        local,
        mesh=mesh,
        in_specs=(P("feat", "blk"), P("feat", "blk"), P("blk"), P("blk")),
        out_specs=(P("blk"), P(("blk", "feat")), P(("blk", "feat"), None)),
        check_vma=False,
    )
```

```python
import functools

import jax
import jax.numpy as jnp
from jax import lax
from jax.experimental import pallas as pl
from jax.experimental.pallas import tpu as pltpu
from jax.sharding import PartitionSpec as P

HOPS = 4
EXTRA = 16
CHUNK = 512
STAT = 128


def shifted(block, distance):
    size = lax.axis_size("blk")
    return lax.ppermute(block, "blk", [(i, (i + distance) % size) for i in range(size)])


def swapped(block, mask):
    size = lax.axis_size("feat")
    return lax.ppermute(block, "feat", [(i, i ^ mask) for i in range(size)])


def three_terms(value):
    high = value.astype(jnp.bfloat16).astype(jnp.float32)
    rest = value - high
    middle = rest.astype(jnp.bfloat16).astype(jnp.float32)
    return high, middle, rest - middle


def stat_lanes(lse):
    high, middle, low = three_terms(lse)
    lane = lax.broadcasted_iota(jnp.int32, (lse.shape[0], STAT), 1)
    return jnp.where(lane == 0, high, jnp.where(lane == 1, middle, jnp.where(lane == 2, low, 0.0)))


def stat_sum(packed):
    features = packed.shape[1] - STAT
    return jnp.sum(packed[:, features : features + 3], axis=1, keepdims=True)


def joined(lses):
    top = functools.reduce(jnp.maximum, lses)
    weights = [jnp.exp(lse - top) for lse in lses]
    total = functools.reduce(jnp.add, weights)
    return [weight / total for weight in weights], top + jnp.log(total)


def split_kernel(cent, pot, out):
    depth, quarter = cent.shape[0], out.shape[2]
    for at in range(out.shape[0]):
        cut = slice(at * quarter, (at + 1) * quarter)
        out[at, :depth, :] = cent[:, cut]
        high, middle, low = three_terms(pot[:, cut])
        row = lax.broadcasted_iota(jnp.int32, (EXTRA, quarter), 0)
        rows = jnp.where(row == 0, high, jnp.where(row == 1, middle, jnp.where(row == 2, low, 0.0)))
        out[at, depth:, :] = rows.astype(jnp.bfloat16)


def split_panel(centroids, col_pot):
    depth, width = centroids.shape
    return pl.pallas_call(
        split_kernel,
        out_shape=jax.ShapeDtypeStruct((4, depth + EXTRA, width // 4), centroids.dtype),
        compiler_params=pltpu.CompilerParams(vmem_limit_bytes=4 * 2**20),
        name="split_panel",
    )(centroids, col_pot[None, :])


def hand_on_kernel(value, *refs):
    refs[-1][...] = value[...]


def hand_on(value, arrays, name):
    return pl.pallas_call(
        hand_on_kernel,
        in_specs=[pl.BlockSpec(memory_space=pltpu.VMEM)] + [pl.BlockSpec(memory_space=pl.ANY)] * len(arrays),
        out_shape=jax.ShapeDtypeStruct(value.shape, value.dtype),
        compiler_params=pltpu.CompilerParams(vmem_limit_bytes=2**20),
        cost_estimate=pl.CostEstimate(flops=10**11, bytes_accessed=2**28, transcendentals=10**8),
        name=name,
    )(value, *arrays)


def pair_kernel(scale, first, *refs):
    pts = refs[:4]
    panel, row_pot = refs[4:6]
    packed, row_out, scores = refs[-3:]
    row_in = None if first else refs[6]
    arrived = refs[6 if first else 7 : -3]
    depth, count = pts[0].shape
    features = 4 * depth
    member = lax.axis_index("feat")
    cols = []
    squares = None
    for m in range(4):
        turned = panel[member ^ m].T
        cols.append(turned[:, :depth])
        wide = turned[:, :depth].astype(jnp.float32)
        part = jnp.sum(wide * wide, axis=1, keepdims=True)
        squares = part if squares is None else squares + part
    extra = turned[:, depth : depth + 3].astype(jnp.float32)
    potential = jnp.sum(extra, axis=1, keepdims=True)
    bias = (-0.5 * scale) * squares
    top = None
    for at in range(0, count, CHUNK):
        here = pl.ds(at, CHUNK)
        score = None
        for m in range(4):
            part = jnp.dot(cols[m], pts[m][:, here], preferred_element_type=jnp.float32)
            score = part if score is None else score + part
        score = score * scale + bias
        row_terms = score + potential
        row_max = jnp.max(row_terms, axis=0, keepdims=True)
        row_sum = jnp.sum(jnp.exp(row_terms - row_max), axis=0, keepdims=True)
        row_part = row_max + jnp.log(row_sum)
        if not first:
            before = row_in[:, here]
            larger = jnp.maximum(before, row_part)
            row_part = larger + jnp.log(jnp.exp(before - larger) + jnp.exp(row_part - larger))
        row_out[:, here] = row_part
        col_terms = score - row_pot[:, here]
        scores[:, here] = col_terms
        for j in range(0, CHUNK, 128):
            lane_part = col_terms[:, j : j + 128]
            top = lane_part if top is None else jnp.maximum(top, lane_part)
    col_max = jnp.max(top, axis=1, keepdims=True)
    lane_sum = None
    acc = [None] * 4
    for at in range(0, count, CHUNK):
        here = pl.ds(at, CHUNK)
        expo = jnp.exp(scores[:, here] - col_max)
        for j in range(0, CHUNK, 128):
            lane_part = expo[:, j : j + 128]
            lane_sum = lane_part if lane_sum is None else lane_sum + lane_part
        weight = expo.astype(jnp.bfloat16)
        for m in range(4):
            part = lax.dot_general(
                weight, pts[m][:, here], (((1,), (1,)), ((), ())), preferred_element_type=jnp.float32
            )
            acc[m] = part if acc[m] is None else acc[m] + part
    col_sum = jnp.sum(lane_sum, axis=1, keepdims=True)
    lse = col_max + jnp.log(col_sum)
    scales, lse = joined([lse] + [stat_sum(ref) for ref in arrived])
    scales[0] = scales[0] / col_sum
    for m in range(4):
        cut = slice(depth * m, depth * (m + 1))
        mean = acc[m] * scales[0]
        for scaling, ref in zip(scales[1:], arrived):
            mean = mean + ref[:, cut] * scaling
        packed[:, cut] = mean
    packed[:, features:] = stat_lanes(lse)


def pair(points, panel, row_pot, row_in, name, arrived=()):
    depth, count = points[0].shape
    features = 4 * depth
    quarter = panel.shape[2]
    operands = (*points, panel, row_pot)
    operands += () if row_in is None else (row_in,)
    operands += tuple(arrived)
    return pl.pallas_call(
        functools.partial(pair_kernel, 1.0 / (0.02 * features), row_in is None),
        out_shape=(
            jax.ShapeDtypeStruct((quarter, features + STAT), jnp.float32),
            jax.ShapeDtypeStruct((1, count), jnp.float32),
        ),
        scratch_shapes=[pltpu.VMEM((quarter, count), jnp.float32)],
        compiler_params=pltpu.CompilerParams(vmem_limit_bytes=12 * 2**20),
        cost_estimate=pl.CostEstimate(flops=1, bytes_accessed=1, transcendentals=0),
        name=name,
    )(*operands)


def half(packed):
    return packed.astype(jnp.float16)


def whole(packed):
    return packed.astype(jnp.float32)


def merge_kernel(*refs):
    parts, mean_out, lse_out = refs[:-2], refs[-2], refs[-1]
    features = mean_out.shape[1]
    scales, lse = joined([stat_sum(part) for part in parts])
    mean = functools.reduce(jnp.add, [part[:, :features] * scaling for part, scaling in zip(parts, scales)])
    lse_out[...] = jnp.broadcast_to(lse, (lse.shape[0], lse.shape[0])).T[:1, :]
    member = lax.axis_index("feat")
    depth = features // 4
    for at in range(4):

        @pl.when(member == at)
        def _():
            for m in range(4):
                mean_out[:, depth * (m ^ at) : depth * ((m ^ at) + 1)] = mean[:, depth * m : depth * (m + 1)]


def merge(parts):
    quarter, width = parts[0].shape
    return pl.pallas_call(
        merge_kernel,
        out_shape=(
            jax.ShapeDtypeStruct((quarter, width - STAT), jnp.float32),
            jax.ShapeDtypeStruct((1, quarter), jnp.float32),
        ),
        compiler_params=pltpu.CompilerParams(vmem_limit_bytes=8 * 2**20),
        cost_estimate=pl.CostEstimate(flops=1, bytes_accessed=1, transcendentals=0),
        name="merge_last",
    )(*parts)


def rows_kernel(parts, out):
    top = jnp.max(parts[...], axis=0, keepdims=True)
    out[...] = top + jnp.log(jnp.sum(jnp.exp(parts[...] - top), axis=0, keepdims=True))


def rows_merged(parts):
    return pl.pallas_call(
        rows_kernel,
        out_shape=jax.ShapeDtypeStruct((1, parts.shape[1]), jnp.float32),
        compiler_params=pltpu.CompilerParams(vmem_limit_bytes=2**20),
        cost_estimate=pl.CostEstimate(flops=1, bytes_accessed=1, transcendentals=0),
        name="rows_merged",
    )(parts)[0]


def after(value, earlier):
    return lax.optimization_barrier((value, earlier))[0]


def local(points, centroids, col_pot, row_pot):
    panel0 = lax.all_to_all(split_panel(centroids, col_pot), "feat", split_axis=0, concat_axis=0, tiled=True)
    panel4 = shifted(panel0, 4)
    across = swapped(after(points, panel0), 2)
    panel1 = shifted(panel0, 1)
    beside = swapped(after(points, panel0), 1)
    panel2 = shifted(panel1, 1)
    pot = hand_on(row_pot[None, :], (panel4,), "far_panel")
    panel3 = shifted(after(panel4, pot), -1)
    diagonal = swapped(across, 1)
    pot = hand_on(pot, (panel3, panel2), "all_panels")
    full = (points, beside, across, diagonal)
    part4, rows = pair(full, panel4, pot, None, "pair4")
    back4 = whole(shifted(half(part4), -4))
    part3, rows = pair(full, panel3, pot, rows, "pair3")
    next3 = whole(shifted(half(part3), -1))
    part1, rows = pair(full, panel1, pot, rows, "pair1")
    back1 = whole(shifted(half(part1), -1))
    part0, rows = pair(full, panel0, pot, rows, "pair0")
    part2, rows = pair(full, panel2, pot, rows, "pair2", (next3,))
    back2 = whole(shifted(half(part2), -2))
    row_lse = rows_merged(lax.all_gather(rows, "feat", axis=0, tiled=True))
    mean, col_lse = merge((part0, back1, back4, back2))
    return (row_lse, col_lse[0], mean)


def solution(mesh):
    return jax.shard_map(
        local,
        mesh=mesh,
        in_specs=(P("feat", "blk"), P("feat", "blk"), P("blk"), P("blk")),
        out_specs=(P("blk"), P(("blk", "feat")), P(("blk", "feat"), None)),
        check_vma=False,
    )
```

```python
import functools

import jax
import jax.numpy as jnp
from jax import lax
from jax.experimental import pallas as pl
from jax.experimental.pallas import tpu as pltpu
from jax.sharding import PartitionSpec as P

ROW = 8
EXTRA = 16
CHUNK = 512
STAT = 16


def shifted(block, distance):
    size = lax.axis_size("blk")
    return lax.ppermute(block, "blk", [(i, (i + distance) % size) for i in range(size)])


def half_way(size):
    return [i // ROW * ROW + (i + 2) % ROW for i in range(size)]


def four_back_first(block):
    size = lax.axis_size("blk")
    return lax.ppermute(block, "blk", list(enumerate(half_way(size))))


def four_back_second(block):
    size = lax.axis_size("blk")
    return lax.ppermute(block, "blk", [(at, (i - 4) % size) for i, at in enumerate(half_way(size))])


def swapped(block, mask):
    size = lax.axis_size("feat")
    return lax.ppermute(block, "feat", [(i, i ^ mask) for i in range(size)])


def three_terms(value):
    high = value.astype(jnp.bfloat16).astype(jnp.float32)
    rest = value - high
    middle = rest.astype(jnp.bfloat16).astype(jnp.float32)
    return high, middle, rest - middle


def stat_rows(lse):
    count = lse.shape[0]
    high, middle, low = three_terms(jnp.broadcast_to(lse, (count, count)).T[:STAT])
    row = lax.broadcasted_iota(jnp.int32, (STAT, count), 0)
    rows = jnp.where(row == 0, high, jnp.where(row == 1, middle, jnp.where(row == 2, low, 0.0)))
    return rows


def stat_sum(packed):
    count = packed.shape[0] - STAT
    total = jnp.sum(packed[count : count + 3, :count], axis=0, keepdims=True)
    return jnp.broadcast_to(total, (count, count)).T[:, :1]


def joined(lses):
    top = functools.reduce(jnp.maximum, lses)
    weights = [jnp.exp(lse - top) for lse in lses]
    total = functools.reduce(jnp.add, weights)
    return [weight / total for weight in weights], top + jnp.log(total)


def split_kernel(cent, pot, out, pots, sems):
    depth, quarter = cent.shape[0], out.shape[2]
    parts = out.shape[0]
    copies = [pltpu.make_async_copy(pot, pots, sems.at[parts])]
    for at in range(parts):
        columns = cent.at[:, pl.ds(at * quarter, quarter)]
        copies.append(pltpu.make_async_copy(columns, out.at[at, pl.ds(0, depth), :], sems.at[at]))
    for copy in copies:
        copy.start()
    copies[0].wait()
    for at in range(parts):
        high, middle, low = three_terms(pots[:, at * quarter : (at + 1) * quarter])
        row = lax.broadcasted_iota(jnp.int32, (EXTRA, quarter), 0)
        rows = jnp.where(row == 0, high, jnp.where(row == 1, middle, jnp.where(row == 2, low, 0.0)))
        out[at, depth:, :] = rows.astype(jnp.bfloat16)
    for copy in copies[1:]:
        copy.wait()


def split_panel(centroids, col_pot):
    depth, width = centroids.shape
    return pl.pallas_call(
        split_kernel,
        in_specs=[pl.BlockSpec(memory_space=pl.ANY)] * 2,
        out_shape=jax.ShapeDtypeStruct((4, depth + EXTRA, width // 4), centroids.dtype),
        scratch_shapes=[pltpu.VMEM((1, width), jnp.float32), pltpu.SemaphoreType.DMA((5,))],
        compiler_params=pltpu.CompilerParams(vmem_limit_bytes=32 * 2**20),
        name="split_panel",
    )(centroids, col_pot[None, :])


def hand_on_kernel(value, *refs):
    refs[-1][...] = value[...]


def hand_on(value, arrays, name):
    return pl.pallas_call(
        hand_on_kernel,
        in_specs=[pl.BlockSpec(memory_space=pltpu.VMEM)] + [pl.BlockSpec(memory_space=pl.ANY)] * len(arrays),
        out_shape=jax.ShapeDtypeStruct(value.shape, value.dtype),
        compiler_params=pltpu.CompilerParams(vmem_limit_bytes=2**20),
        cost_estimate=pl.CostEstimate(flops=10**11, bytes_accessed=2**28, transcendentals=10**8),
        name=name,
    )(value, *arrays)


def pair_kernel(scale, panels, first, *refs):
    pts, panel_refs, row_pot = refs[:4], refs[4 : 4 + panels], refs[4 + panels]
    outs, row_out, scores = refs[-2 - panels : -2], refs[-2], refs[-1]
    rest = refs[5 + panels : -2 - panels]
    row_in, arrived = (None, rest) if first else (rest[0], rest[1:])
    depth, count = pts[0].shape
    features = 4 * depth
    quarter = outs[0].shape[0] - STAT
    member = lax.axis_index("feat")
    cols = []
    squares = None
    for m in range(4):
        turned = jnp.concatenate([panel[member ^ m].T for panel in panel_refs], axis=0)
        cols.append(turned[:, :depth])
        wide = turned[:, :depth].astype(jnp.float32)
        part = jnp.sum(wide * wide, axis=1, keepdims=True)
        squares = part if squares is None else squares + part
    extra = turned[:, depth : depth + 3].astype(jnp.float32)
    potential = jnp.sum(extra, axis=1, keepdims=True)
    bias = (-0.5 * scale) * squares
    top = None
    for at in range(0, count, CHUNK):
        here = pl.ds(at, CHUNK)
        score = None
        for m in range(4):
            part = jnp.dot(cols[m], pts[m][:, here], preferred_element_type=jnp.float32)
            score = part if score is None else score + part
        score = score * scale + bias
        row_terms = score + potential
        row_max = jnp.max(row_terms, axis=0, keepdims=True)
        row_sum = jnp.sum(jnp.exp(row_terms - row_max), axis=0, keepdims=True)
        row_part = row_max + jnp.log(row_sum)
        if not first:
            before = row_in[:, here]
            larger = jnp.maximum(before, row_part)
            row_part = larger + jnp.log(jnp.exp(before - larger) + jnp.exp(row_part - larger))
        row_out[:, here] = row_part
        col_terms = score - row_pot[:, here]
        scores[:, here] = col_terms
        for j in range(0, CHUNK, 128):
            lane_part = col_terms[:, j : j + 128]
            top = lane_part if top is None else jnp.maximum(top, lane_part)
    col_max = jnp.max(top, axis=1, keepdims=True)
    lane_sum = None
    acc = [None] * 4
    for at in range(0, count, CHUNK):
        here = pl.ds(at, CHUNK)
        expo = jnp.exp(scores[:, here] - col_max)
        for j in range(0, CHUNK, 128):
            lane_part = expo[:, j : j + 128]
            lane_sum = lane_part if lane_sum is None else lane_sum + lane_part
        weight = expo.astype(jnp.bfloat16)
        for m in range(4):
            part = lax.dot_general(
                weight, pts[m][:, here], (((1,), (1,)), ((), ())), preferred_element_type=jnp.float32
            )
            acc[m] = part if acc[m] is None else acc[m] + part
    col_sum = jnp.sum(lane_sum, axis=1, keepdims=True)
    lse = col_max + jnp.log(col_sum)
    shares, lse = joined([lse] + [stat_sum(ref) for ref in arrived])
    shares[0] = shares[0] / col_sum
    for i, packed in enumerate(outs):
        mine = slice(i * quarter, (i + 1) * quarter)
        for m in range(4):
            cut = slice(depth * m, depth * (m + 1))
            mean = acc[m][mine] * shares[0][mine]
            for share, ref in zip(shares[1:], arrived):
                mean = mean + ref[:quarter, cut] * share
            packed[:quarter, cut] = mean
        packed[quarter:, :] = jnp.zeros((STAT, features), jnp.float32)
        packed[quarter:, :quarter] = stat_rows(lse[mine])


def pair(points, panels, row_pot, row_in, name, arrived=()):
    depth, count = points[0].shape
    features = 4 * depth
    quarter = panels[0].shape[2]
    operands = (*points, *panels, row_pot)
    operands += () if row_in is None else (row_in,)
    operands += tuple(arrived)
    return pl.pallas_call(
        functools.partial(pair_kernel, 1.0 / (0.02 * features), len(panels), row_in is None),
        out_shape=(
            *[jax.ShapeDtypeStruct((quarter + STAT, features), jnp.float32)] * len(panels),
            jax.ShapeDtypeStruct((1, count), jnp.float32),
        ),
        scratch_shapes=[pltpu.VMEM((quarter * len(panels), count), jnp.float32)],
        compiler_params=pltpu.CompilerParams(vmem_limit_bytes=16 * 2**20),
        cost_estimate=pl.CostEstimate(flops=1, bytes_accessed=1, transcendentals=0),
        name=name,
    )(*operands)


def half(packed):
    return packed.astype(jnp.float16)


def whole(packed):
    return packed.astype(jnp.float32)


def merge_kernel(*refs):
    parts, mean_out, lse_out = refs[:-2], refs[-2], refs[-1]
    features = mean_out.shape[1]
    scales, lse = joined([stat_sum(part) for part in parts])
    count = mean_out.shape[0]
    mean = functools.reduce(jnp.add, [part[:count] * scaling for part, scaling in zip(parts, scales)])
    lse_out[...] = jnp.broadcast_to(lse, (lse.shape[0], lse.shape[0])).T[:1, :]
    member = lax.axis_index("feat")
    depth = features // 4
    for at in range(4):

        @pl.when(member == at)
        def _():
            for m in range(4):
                mean_out[:, depth * (m ^ at) : depth * ((m ^ at) + 1)] = mean[:, depth * m : depth * (m + 1)]


def merge(parts):
    rows, width = parts[0].shape
    quarter = rows - STAT
    return pl.pallas_call(
        merge_kernel,
        out_shape=(
            jax.ShapeDtypeStruct((quarter, width), jnp.float32),
            jax.ShapeDtypeStruct((1, quarter), jnp.float32),
        ),
        compiler_params=pltpu.CompilerParams(vmem_limit_bytes=8 * 2**20),
        cost_estimate=pl.CostEstimate(flops=1, bytes_accessed=1, transcendentals=0),
        name="merge_last",
    )(*parts)


def rows_kernel(parts, out):
    top = jnp.max(parts[...], axis=0, keepdims=True)
    out[...] = top + jnp.log(jnp.sum(jnp.exp(parts[...] - top), axis=0, keepdims=True))


def rows_merged(parts):
    return pl.pallas_call(
        rows_kernel,
        out_shape=jax.ShapeDtypeStruct((1, parts.shape[1]), jnp.float32),
        compiler_params=pltpu.CompilerParams(vmem_limit_bytes=2**20),
        cost_estimate=pl.CostEstimate(flops=1, bytes_accessed=1, transcendentals=0),
        name="rows_merged",
    )(parts)[0]


def after(value, earlier):
    return lax.optimization_barrier((value, earlier))[0]


def local(points, centroids, col_pot, row_pot):
    panel0 = lax.all_to_all(split_panel(centroids, col_pot), "feat", split_axis=0, concat_axis=0, tiled=True)
    across = swapped(after(points, panel0), 2)
    panel4 = shifted(panel0, 4)
    panel1 = shifted(panel0, 1)
    beside = swapped(after(points, panel0), 1)
    panel2 = shifted(panel1, 1)
    panel3 = shifted(panel4, -1)
    diagonal = swapped(across, 1)
    pot = hand_on(row_pot[None, :], (panel3, panel2), "all_panels")
    full = (points, beside, across, diagonal)
    part3, part4, rows = pair(full, (panel3, panel4), pot, None, "pair34")
    under_way = four_back_first(half(part4))
    next3 = whole(shifted(half(part3), -1))
    part1, part0, rows = pair(full, (panel1, panel0), pot, rows, "pair10")
    back1 = whole(shifted(half(part1), -1))
    back4 = whole(four_back_second(under_way))
    part2, rows = pair(full, (panel2,), pot, rows, "pair2", (next3,))
    back2 = whole(shifted(half(part2), -2))
    row_lse = rows_merged(lax.all_gather(rows, "feat", axis=0, tiled=True))
    mean, col_lse = merge((part0, back1, back4, back2))
    return (row_lse, col_lse[0], mean)


def solution(mesh):
    return jax.shard_map(
        local,
        mesh=mesh,
        in_specs=(P("feat", "blk"), P("feat", "blk"), P("blk"), P("blk")),
        out_specs=(P("blk"), P(("blk", "feat")), P(("blk", "feat"), None)),
        check_vma=False,
    )
```

```python
import functools

import jax
import jax.numpy as jnp
from jax import lax
from jax.experimental import pallas as pl
from jax.experimental.pallas import tpu as pltpu
from jax.sharding import PartitionSpec as P

ROW = 8
EXTRA = 16
CHUNK = 512
STAT = 16


def shifted(block, distance):
    size = lax.axis_size("blk")
    return lax.ppermute(block, "blk", [(i, (i + distance) % size) for i in range(size)])


def half_way(size):
    return [i // ROW * ROW + (i + 2) % ROW for i in range(size)]


def four_back_first(block):
    size = lax.axis_size("blk")
    return lax.ppermute(block, "blk", list(enumerate(half_way(size))))


def four_back_second(block):
    size = lax.axis_size("blk")
    return lax.ppermute(block, "blk", [(at, (i - 4) % size) for i, at in enumerate(half_way(size))])


def swapped(block, mask):
    size = lax.axis_size("feat")
    return lax.ppermute(block, "feat", [(i, i ^ mask) for i in range(size)])


def three_terms(value):
    high = value.astype(jnp.bfloat16).astype(jnp.float32)
    rest = value - high
    middle = rest.astype(jnp.bfloat16).astype(jnp.float32)
    return high, middle, rest - middle


def stat_rows(lse):
    count = lse.shape[0]
    high, middle, low = three_terms(jnp.broadcast_to(lse, (count, count)).T[:STAT])
    row = lax.broadcasted_iota(jnp.int32, (STAT, count), 0)
    rows = jnp.where(row == 0, high, jnp.where(row == 1, middle, jnp.where(row == 2, low, 0.0)))
    return rows


def stat_sum(packed):
    count = packed.shape[0] - STAT
    total = jnp.sum(packed[count : count + 3, :count], axis=0, keepdims=True)
    return jnp.broadcast_to(total, (count, count)).T[:, :1]


def joined(lses):
    top = functools.reduce(jnp.maximum, lses)
    weights = [jnp.exp(lse - top) for lse in lses]
    total = functools.reduce(jnp.add, weights)
    return [weight / total for weight in weights], top + jnp.log(total)


def split_kernel(cent, pot, out, pots, sems):
    depth, quarter = cent.shape[0], out.shape[2]
    parts = out.shape[0]
    copies = [pltpu.make_async_copy(pot, pots, sems.at[parts])]
    for at in range(parts):
        columns = cent.at[:, pl.ds(at * quarter, quarter)]
        copies.append(pltpu.make_async_copy(columns, out.at[at, pl.ds(0, depth), :], sems.at[at]))
    for copy in copies:
        copy.start()
    copies[0].wait()
    for at in range(parts):
        high, middle, low = three_terms(pots[:, at * quarter : (at + 1) * quarter])
        row = lax.broadcasted_iota(jnp.int32, (EXTRA, quarter), 0)
        rows = jnp.where(row == 0, high, jnp.where(row == 1, middle, jnp.where(row == 2, low, 0.0)))
        out[at, depth:, :] = rows.astype(jnp.bfloat16)
    for copy in copies[1:]:
        copy.wait()


def split_panel(centroids, col_pot):
    depth, width = centroids.shape
    return pl.pallas_call(
        split_kernel,
        in_specs=[pl.BlockSpec(memory_space=pl.ANY)] * 2,
        out_shape=jax.ShapeDtypeStruct((4, depth + EXTRA, width // 4), centroids.dtype),
        scratch_shapes=[pltpu.VMEM((1, width), jnp.float32), pltpu.SemaphoreType.DMA((5,))],
        compiler_params=pltpu.CompilerParams(vmem_limit_bytes=32 * 2**20),
        name="split_panel",
    )(centroids, col_pot[None, :])


def hand_on_kernel(value, *refs):
    refs[-1][...] = value[...]


def hand_on(value, arrays, name):
    return pl.pallas_call(
        hand_on_kernel,
        in_specs=[pl.BlockSpec(memory_space=pltpu.VMEM)] + [pl.BlockSpec(memory_space=pl.ANY)] * len(arrays),
        out_shape=jax.ShapeDtypeStruct(value.shape, value.dtype),
        compiler_params=pltpu.CompilerParams(vmem_limit_bytes=2**20),
        cost_estimate=pl.CostEstimate(flops=10**11, bytes_accessed=2**28, transcendentals=10**8),
        name=name,
    )(value, *arrays)


def pair_kernel(scale, panels, first, *refs):
    pts, panel_refs, row_pot = refs[:4], refs[4 : 4 + panels], refs[4 + panels]
    outs, row_out, scores = refs[-2 - panels : -2], refs[-2], refs[-1]
    rest = refs[5 + panels : -2 - panels]
    row_in, arrived = (None, rest) if first else (rest[0], rest[1:])
    depth, count = pts[0].shape
    features = 4 * depth
    quarter = outs[0].shape[0] - STAT
    member = lax.axis_index("feat")
    cols = []
    squares = None
    for m in range(4):
        turned = jnp.concatenate([panel[member ^ m].T for panel in panel_refs], axis=0)
        cols.append(turned[:, :depth])
        wide = turned[:, :depth].astype(jnp.float32)
        part = jnp.sum(wide * wide, axis=1, keepdims=True)
        squares = part if squares is None else squares + part
    extra = turned[:, depth : depth + 3].astype(jnp.float32)
    potential = jnp.sum(extra, axis=1, keepdims=True)
    bias = (-0.5 * scale) * squares
    top = None
    for at in range(0, count, CHUNK):
        here = pl.ds(at, CHUNK)
        score = None
        for m in range(4):
            part = jnp.dot(cols[m], pts[m][:, here], preferred_element_type=jnp.float32)
            score = part if score is None else score + part
        score = score * scale + bias
        row_terms = score + potential
        row_max = jnp.max(row_terms, axis=0, keepdims=True)
        row_sum = jnp.sum(jnp.exp(row_terms - row_max), axis=0, keepdims=True)
        row_part = row_max + jnp.log(row_sum)
        if not first:
            before = row_in[:, here]
            larger = jnp.maximum(before, row_part)
            row_part = larger + jnp.log(jnp.exp(before - larger) + jnp.exp(row_part - larger))
        row_out[:, here] = row_part
        col_terms = score - row_pot[:, here]
        scores[:, here] = col_terms
        for j in range(0, CHUNK, 128):
            lane_part = col_terms[:, j : j + 128]
            top = lane_part if top is None else jnp.maximum(top, lane_part)
    col_max = jnp.max(top, axis=1, keepdims=True)
    lane_sum = None
    acc = [None] * 4
    for at in range(0, count, CHUNK):
        here = pl.ds(at, CHUNK)
        expo = jnp.exp(scores[:, here] - col_max)
        for j in range(0, CHUNK, 128):
            lane_part = expo[:, j : j + 128]
            lane_sum = lane_part if lane_sum is None else lane_sum + lane_part
        weight = expo.astype(jnp.bfloat16)
        for m in range(4):
            part = lax.dot_general(
                weight, pts[m][:, here], (((1,), (1,)), ((), ())), preferred_element_type=jnp.float32
            )
            acc[m] = part if acc[m] is None else acc[m] + part
    col_sum = jnp.sum(lane_sum, axis=1, keepdims=True)
    lse = col_max + jnp.log(col_sum)
    shares, lse = joined([lse] + [stat_sum(ref) for ref in arrived])
    shares[0] = shares[0] / col_sum
    for i, packed in enumerate(outs):
        mine = slice(i * quarter, (i + 1) * quarter)
        for m in range(4):
            cut = slice(depth * m, depth * (m + 1))
            mean = acc[m][mine] * shares[0][mine]
            for share, ref in zip(shares[1:], arrived):
                mean = mean + ref[:quarter, cut] * share
            packed[:quarter, cut] = mean
        packed[quarter:, :] = jnp.zeros((STAT, features), jnp.float32)
        packed[quarter:, :quarter] = stat_rows(lse[mine])


def pair(points, panels, row_pot, row_in, name, arrived=()):
    depth, count = points[0].shape
    features = 4 * depth
    quarter = panels[0].shape[2]
    operands = (*points, *panels, row_pot)
    operands += () if row_in is None else (row_in,)
    operands += tuple(arrived)
    return pl.pallas_call(
        functools.partial(pair_kernel, 1.0 / (0.02 * features), len(panels), row_in is None),
        out_shape=(
            *[jax.ShapeDtypeStruct((quarter + STAT, features), jnp.float32)] * len(panels),
            jax.ShapeDtypeStruct((1, count), jnp.float32),
        ),
        scratch_shapes=[pltpu.VMEM((quarter * len(panels), count), jnp.float32)],
        compiler_params=pltpu.CompilerParams(vmem_limit_bytes=16 * 2**20),
        cost_estimate=pl.CostEstimate(flops=1, bytes_accessed=1, transcendentals=0),
        name=name,
    )(*operands)


def half(packed):
    return packed.astype(jnp.float16)


def whole(packed):
    return packed.astype(jnp.float32)


def merge_kernel(*refs):
    parts, mean_out, lse_out = refs[:-2], refs[-2], refs[-1]
    features = mean_out.shape[1]
    scales, lse = joined([stat_sum(part) for part in parts])
    count = mean_out.shape[0]
    mean = functools.reduce(jnp.add, [part[:count] * scaling for part, scaling in zip(parts, scales)])
    lse_out[...] = jnp.broadcast_to(lse, (lse.shape[0], lse.shape[0])).T[:1, :]
    member = lax.axis_index("feat")
    depth = features // 4
    for at in range(4):

        @pl.when(member == at)
        def _():
            for m in range(4):
                mean_out[:, depth * (m ^ at) : depth * ((m ^ at) + 1)] = mean[:, depth * m : depth * (m + 1)]


def merge(parts):
    rows, width = parts[0].shape
    quarter = rows - STAT
    return pl.pallas_call(
        merge_kernel,
        out_shape=(
            jax.ShapeDtypeStruct((quarter, width), jnp.float32),
            jax.ShapeDtypeStruct((1, quarter), jnp.float32),
        ),
        compiler_params=pltpu.CompilerParams(vmem_limit_bytes=8 * 2**20),
        cost_estimate=pl.CostEstimate(flops=1, bytes_accessed=1, transcendentals=0),
        name="merge_last",
    )(*parts)


def blend_kernel(first, second, out):
    count = out.shape[0] - STAT
    shares, lse = joined([stat_sum(first), stat_sum(second)])
    out[:count] = first[:count] * shares[0] + second[:count] * shares[1]
    out[count:, :] = jnp.zeros((STAT, out.shape[1]), jnp.float32)
    out[count:, :count] = stat_rows(lse)


def blend(first, second):
    return pl.pallas_call(
        blend_kernel,
        out_shape=jax.ShapeDtypeStruct(first.shape, jnp.float32),
        compiler_params=pltpu.CompilerParams(vmem_limit_bytes=4 * 2**20),
        cost_estimate=pl.CostEstimate(flops=1, bytes_accessed=1, transcendentals=0),
        name="blend",
    )(first, second)


def rows_kernel(parts, out):
    top = jnp.max(parts[...], axis=0, keepdims=True)
    out[...] = top + jnp.log(jnp.sum(jnp.exp(parts[...] - top), axis=0, keepdims=True))


def rows_merged(parts):
    return pl.pallas_call(
        rows_kernel,
        out_shape=jax.ShapeDtypeStruct((1, parts.shape[1]), jnp.float32),
        compiler_params=pltpu.CompilerParams(vmem_limit_bytes=2**20),
        cost_estimate=pl.CostEstimate(flops=1, bytes_accessed=1, transcendentals=0),
        name="rows_merged",
    )(parts)[0]


def after(value, earlier):
    return lax.optimization_barrier((value, earlier))[0]


def local(points, centroids, col_pot, row_pot):
    panel0 = lax.all_to_all(split_panel(centroids, col_pot), "feat", split_axis=0, concat_axis=0, tiled=True)
    across = swapped(after(points, panel0), 2)
    panel4 = shifted(panel0, 4)
    panel1 = shifted(panel0, 1)
    beside = swapped(after(points, panel0), 1)
    panel2 = shifted(panel1, 1)
    panel3 = shifted(panel4, -1)
    diagonal = swapped(across, 1)
    pot = hand_on(row_pot[None, :], (panel3, panel2), "all_panels")
    full = (points, beside, across, diagonal)
    part3, part4, rows = pair(full, (panel3, panel4), pot, None, "pair34")
    under_way = four_back_first(half(part4))
    next3 = whole(shifted(half(part3), -1))
    part1, part0, part2, rows = pair(full, (panel1, panel0, panel2), pot, rows, "pair102")
    back1 = whole(shifted(half(part1), -1))
    back4 = whole(four_back_second(under_way))
    back2 = whole(shifted(half(blend(part2, next3)), -2))
    row_lse = rows_merged(lax.all_gather(rows, "feat", axis=0, tiled=True))
    mean, col_lse = merge((part0, back1, back4, back2))
    return (row_lse, col_lse[0], mean)


def solution(mesh):
    return jax.shard_map(
        local,
        mesh=mesh,
        in_specs=(P("feat", "blk"), P("feat", "blk"), P("blk"), P("blk")),
        out_specs=(P("blk"), P(("blk", "feat")), P(("blk", "feat"), None)),
        check_vma=False,
    )
```

```python
import functools

import jax
import jax.numpy as jnp
from jax import lax
from jax.experimental import pallas as pl
from jax.experimental.pallas import tpu as pltpu
from jax.sharding import PartitionSpec as P

ROW = 8
EXTRA = 16
CHUNK = 512
STAT = 8


def shifted(block, distance):
    size = lax.axis_size("blk")
    return lax.ppermute(block, "blk", [(i, (i + distance) % size) for i in range(size)])


def half_way(size):
    return [i // ROW * ROW + (i + 2) % ROW for i in range(size)]


def four_back_first(block):
    size = lax.axis_size("blk")
    return lax.ppermute(block, "blk", list(enumerate(half_way(size))))


def four_back_second(block):
    size = lax.axis_size("blk")
    return lax.ppermute(block, "blk", [(at, (i - 4) % size) for i, at in enumerate(half_way(size))])


def swapped(block, mask):
    size = lax.axis_size("feat")
    return lax.ppermute(block, "feat", [(i, i ^ mask) for i in range(size)])


def three_terms(value):
    high = value.astype(jnp.bfloat16).astype(jnp.float32)
    rest = value - high
    middle = rest.astype(jnp.bfloat16).astype(jnp.float32)
    return high, middle, rest - middle


def stat_rows(lse):
    count = lse.shape[0]
    high, middle, low = three_terms(jnp.broadcast_to(lse, (count, count)).T[:STAT])
    row = lax.broadcasted_iota(jnp.int32, (STAT, count), 0)
    rows = jnp.where(row == 0, high, jnp.where(row == 1, middle, jnp.where(row == 2, low, 0.0)))
    return rows


def stat_sum(packed):
    count = packed.shape[0] - STAT
    total = jnp.sum(packed[count : count + 3, :count], axis=0, keepdims=True)
    return jnp.broadcast_to(total, (count, count)).T[:, :1]


def joined(lses):
    top = functools.reduce(jnp.maximum, lses)
    weights = [jnp.exp(lse - top) for lse in lses]
    total = functools.reduce(jnp.add, weights)
    return [weight / total for weight in weights], top + jnp.log(total)


def split_kernel(cent, pot, out, pots, sems):
    depth, quarter = cent.shape[0], out.shape[2]
    parts = out.shape[0]
    copies = [pltpu.make_async_copy(pot, pots, sems.at[parts])]
    for at in range(parts):
        columns = cent.at[:, pl.ds(at * quarter, quarter)]
        copies.append(pltpu.make_async_copy(columns, out.at[at, pl.ds(0, depth), :], sems.at[at]))
    for copy in copies:
        copy.start()
    copies[0].wait()
    for at in range(parts):
        high, middle, low = three_terms(pots[:, at * quarter : (at + 1) * quarter])
        row = lax.broadcasted_iota(jnp.int32, (EXTRA, quarter), 0)
        rows = jnp.where(row == 0, high, jnp.where(row == 1, middle, jnp.where(row == 2, low, 0.0)))
        out[at, depth:, :] = rows.astype(jnp.bfloat16)
    for copy in copies[1:]:
        copy.wait()


def split_panel(centroids, col_pot):
    depth, width = centroids.shape
    return pl.pallas_call(
        split_kernel,
        in_specs=[pl.BlockSpec(memory_space=pl.ANY)] * 2,
        out_shape=jax.ShapeDtypeStruct((4, depth + EXTRA, width // 4), centroids.dtype),
        scratch_shapes=[pltpu.VMEM((1, width), jnp.float32), pltpu.SemaphoreType.DMA((5,))],
        compiler_params=pltpu.CompilerParams(vmem_limit_bytes=32 * 2**20),
        name="split_panel",
    )(centroids, col_pot[None, :])


def hand_on_kernel(value, *refs):
    refs[-1][...] = value[...]


def hand_on(value, arrays, name):
    return pl.pallas_call(
        hand_on_kernel,
        in_specs=[pl.BlockSpec(memory_space=pltpu.VMEM)] + [pl.BlockSpec(memory_space=pl.ANY)] * len(arrays),
        out_shape=jax.ShapeDtypeStruct(value.shape, value.dtype),
        compiler_params=pltpu.CompilerParams(vmem_limit_bytes=2**20),
        cost_estimate=pl.CostEstimate(flops=10**11, bytes_accessed=2**28, transcendentals=10**8),
        name=name,
    )(value, *arrays)


def pair_kernel(scale, panels, first, *refs):
    pts, panel_refs, row_pot = refs[:4], refs[4 : 4 + panels], refs[4 + panels]
    outs, row_out, scores = refs[-2 - panels : -2], refs[-2], refs[-1]
    rest = refs[5 + panels : -2 - panels]
    row_in, arrived = (None, rest) if first else (rest[0], rest[1:])
    depth, count = pts[0].shape
    features = 4 * depth
    quarter = outs[0].shape[0] - STAT
    member = lax.axis_index("feat")
    cols = []
    squares = None
    for m in range(4):
        turned = jnp.concatenate([panel[member ^ m].T for panel in panel_refs], axis=0)
        cols.append(turned[:, :depth])
        wide = turned[:, :depth].astype(jnp.float32)
        part = jnp.sum(wide * wide, axis=1, keepdims=True)
        squares = part if squares is None else squares + part
    extra = turned[:, depth : depth + 3].astype(jnp.float32)
    potential = jnp.sum(extra, axis=1, keepdims=True)
    bias = (-0.5 * scale) * squares
    top = None
    for at in range(0, count, CHUNK):
        here = pl.ds(at, CHUNK)
        score = None
        for m in range(4):
            part = jnp.dot(cols[m], pts[m][:, here], preferred_element_type=jnp.float32)
            score = part if score is None else score + part
        score = score * scale + bias
        row_terms = score + potential
        row_max = jnp.max(row_terms, axis=0, keepdims=True)
        row_sum = jnp.sum(jnp.exp(row_terms - row_max), axis=0, keepdims=True)
        row_part = row_max + jnp.log(row_sum)
        if not first:
            before = row_in[:, here]
            larger = jnp.maximum(before, row_part)
            row_part = larger + jnp.log(jnp.exp(before - larger) + jnp.exp(row_part - larger))
        row_out[:, here] = row_part
        col_terms = score - row_pot[:, here]
        scores[:, here] = col_terms
        for j in range(0, CHUNK, 128):
            lane_part = col_terms[:, j : j + 128]
            top = lane_part if top is None else jnp.maximum(top, lane_part)
    col_max = jnp.max(top, axis=1, keepdims=True)
    lane_sum = None
    acc = [None] * 4
    for at in range(0, count, CHUNK):
        here = pl.ds(at, CHUNK)
        expo = jnp.exp(scores[:, here] - col_max)
        for j in range(0, CHUNK, 128):
            lane_part = expo[:, j : j + 128]
            lane_sum = lane_part if lane_sum is None else lane_sum + lane_part
        weight = expo.astype(jnp.bfloat16)
        for m in range(4):
            part = lax.dot_general(
                weight, pts[m][:, here], (((1,), (1,)), ((), ())), preferred_element_type=jnp.float32
            )
            acc[m] = part if acc[m] is None else acc[m] + part
    col_sum = jnp.sum(lane_sum, axis=1, keepdims=True)
    lse = col_max + jnp.log(col_sum)
    shares, lse = joined([lse] + [stat_sum(ref) for ref in arrived])
    shares[0] = shares[0] / col_sum
    for i, packed in enumerate(outs):
        mine = slice(i * quarter, (i + 1) * quarter)
        for m in range(4):
            cut = slice(depth * m, depth * (m + 1))
            mean = acc[m][mine] * shares[0][mine]
            for share, ref in zip(shares[1:], arrived):
                mean = mean + ref[:quarter, cut] * share
            packed[:quarter, cut] = mean
        packed[quarter:, :] = jnp.zeros((STAT, features), jnp.float32)
        packed[quarter:, :quarter] = stat_rows(lse[mine])


def pair(points, panels, row_pot, row_in, name, arrived=()):
    depth, count = points[0].shape
    features = 4 * depth
    quarter = panels[0].shape[2]
    operands = (*points, *panels, row_pot)
    operands += () if row_in is None else (row_in,)
    operands += tuple(arrived)
    return pl.pallas_call(
        functools.partial(pair_kernel, 1.0 / (0.02 * features), len(panels), row_in is None),
        out_shape=(
            *[jax.ShapeDtypeStruct((quarter + STAT, features), jnp.float32)] * len(panels),
            jax.ShapeDtypeStruct((1, count), jnp.float32),
        ),
        scratch_shapes=[pltpu.VMEM((quarter * len(panels), count), jnp.float32)],
        compiler_params=pltpu.CompilerParams(vmem_limit_bytes=16 * 2**20),
        cost_estimate=pl.CostEstimate(flops=1, bytes_accessed=1, transcendentals=0),
        name=name,
    )(*operands)


def half(packed):
    return packed.astype(jnp.float16)


def whole(packed):
    return packed.astype(jnp.float32)


def merge_kernel(*refs):
    parts, mean_out, lse_out = refs[:-2], refs[-2], refs[-1]
    features = mean_out.shape[1]
    scales, lse = joined([stat_sum(part) for part in parts])
    count = mean_out.shape[0]
    mean = functools.reduce(jnp.add, [part[:count] * scaling for part, scaling in zip(parts, scales)])
    lse_out[...] = jnp.broadcast_to(lse, (lse.shape[0], lse.shape[0])).T[:1, :]
    member = lax.axis_index("feat")
    depth = features // 4
    for at in range(4):

        @pl.when(member == at)
        def _():
            for m in range(4):
                mean_out[:, depth * (m ^ at) : depth * ((m ^ at) + 1)] = mean[:, depth * m : depth * (m + 1)]


def merge(parts):
    rows, width = parts[0].shape
    quarter = rows - STAT
    return pl.pallas_call(
        merge_kernel,
        out_shape=(
            jax.ShapeDtypeStruct((quarter, width), jnp.float32),
            jax.ShapeDtypeStruct((1, quarter), jnp.float32),
        ),
        compiler_params=pltpu.CompilerParams(vmem_limit_bytes=8 * 2**20),
        cost_estimate=pl.CostEstimate(flops=1, bytes_accessed=1, transcendentals=0),
        name="merge_last",
    )(*parts)


def blend_kernel(first, second, out):
    count = out.shape[0] - STAT
    shares, lse = joined([stat_sum(first), stat_sum(second)])
    out[:count] = first[:count] * shares[0] + second[:count] * shares[1]
    out[count:, :] = jnp.zeros((STAT, out.shape[1]), jnp.float32)
    out[count:, :count] = stat_rows(lse)


def blend(first, second):
    return pl.pallas_call(
        blend_kernel,
        out_shape=jax.ShapeDtypeStruct(first.shape, jnp.float32),
        compiler_params=pltpu.CompilerParams(vmem_limit_bytes=4 * 2**20),
        cost_estimate=pl.CostEstimate(flops=1, bytes_accessed=1, transcendentals=0),
        name="blend",
    )(first, second)


def rows_kernel(parts, out):
    top = jnp.max(parts[...], axis=0, keepdims=True)
    out[...] = top + jnp.log(jnp.sum(jnp.exp(parts[...] - top), axis=0, keepdims=True))


def rows_merged(parts):
    return pl.pallas_call(
        rows_kernel,
        out_shape=jax.ShapeDtypeStruct((1, parts.shape[1]), jnp.float32),
        compiler_params=pltpu.CompilerParams(vmem_limit_bytes=2**20),
        cost_estimate=pl.CostEstimate(flops=1, bytes_accessed=1, transcendentals=0),
        name="rows_merged",
    )(parts)[0]


def after(value, earlier):
    return lax.optimization_barrier((value, earlier))[0]


def local(points, centroids, col_pot, row_pot):
    panel0 = lax.all_to_all(split_panel(centroids, col_pot), "feat", split_axis=0, concat_axis=0, tiled=True)
    across = swapped(after(points, panel0), 2)
    panel4 = shifted(panel0, 4)
    panel1 = shifted(panel0, 1)
    beside = swapped(after(points, panel0), 1)
    panel2 = shifted(panel1, 1)
    panel3 = shifted(panel4, -1)
    diagonal = swapped(across, 1)
    pot = hand_on(row_pot[None, :], (panel3, panel2), "all_panels")
    full = (points, beside, across, diagonal)
    part3, part4, rows = pair(full, (panel3, panel4), pot, None, "pair34")
    under_way = four_back_first(half(part4))
    next3 = whole(shifted(half(part3), -1))
    part1, part0, part2, rows = pair(full, (panel1, panel0, panel2), pot, rows, "pair102")
    back1 = whole(shifted(half(part1), -1))
    back4 = whole(four_back_second(under_way))
    back2 = whole(shifted(half(blend(part2, next3)), -2))
    row_lse = rows_merged(lax.all_gather(rows, "feat", axis=0, tiled=True))
    mean, col_lse = merge((part0, back1, back4, back2))
    return (row_lse, col_lse[0], mean)


def solution(mesh):
    return jax.shard_map(
        local,
        mesh=mesh,
        in_specs=(P("feat", "blk"), P("feat", "blk"), P("blk"), P("blk")),
        out_specs=(P("blk"), P(("blk", "feat")), P(("blk", "feat"), None)),
        check_vma=False,
    )
```
